32 devices in a mesh: fsdp: 2 (over y), ctx: 4 (over x, core), tp: 4 (over z).
Axes of the slice: x: 2, y: 2, z: 4, core: 2. Of those that a mesh axis runs over, the one named last changes fastest.
Arguments:
- hidden_in: bfloat16 [4, 1024, 2048], P('fsdp', 'ctx'), may hold values from -6 to 6
- lengths: int32 [4], P('fsdp'), may hold values from 256 to 1024, as said below
- routes: int32 [4, 1024, 6], P('fsdp', 'ctx'), may hold values from 0 to 15, all different within a row; in each aligned block of 256 rows (0 to 255, 256 to 511, ..., all dimensions but the last counted through in order) at most 128 rows name the same one
- gate_weights: float32 [4, 1024, 6], P('fsdp', 'ctx'), may hold values from 0.1 to 0.5
- cotangent: bfloat16 [4, 1024, 2048], P('fsdp', 'ctx'), may hold values from -6 to 6
- attn_gain: bfloat16 [2048], P(('fsdp', 'ctx')), may hold values from 0.5 to 1.5
- query_weight: bfloat16 [2048, 3072], P(('fsdp', 'ctx'), 'tp'), may hold values from -0.125 to 0.125
- latent_down: bfloat16 [2048, 576], P(('fsdp', 'ctx')), may hold values from -0.125 to 0.125
- latent_gain: bfloat16 [512], P(('fsdp', 'ctx')), may hold values from 0.5 to 1.5
- latent_up: bfloat16 [512, 4096], P(('fsdp', 'ctx'), 'tp'), may hold values from -0.25 to 0.25
- output_weight: bfloat16 [2048, 2048], P('tp', ('fsdp', 'ctx')), may hold values from -0.375 to 0.375
- ffn_gain: bfloat16 [2048], P(('fsdp', 'ctx')), may hold values from 0.5 to 1.5
- shared_gate_up: bfloat16 [2048, 2, 2816], P(('fsdp', 'ctx'), None, 'tp'), may hold values from -0.125 to 0.125
- shared_down: bfloat16 [2816, 2048], P('tp', ('fsdp', 'ctx')), may hold values from -0.109375 to 0.109375
- expert_gate_up: bfloat16 [2048, 16, 2, 1408], P(('fsdp', 'ctx'), None, None, 'tp'), may hold values from -0.125 to 0.125
- expert_down: bfloat16 [2048, 16, 1408], P(('fsdp', 'ctx'), None, 'tp'), may hold values from -0.15625 to 0.15625
Outputs:
- block_out: bfloat16 [4, 1024, 2048], P('fsdp', 'ctx')
- input_grad: float32 [4, 1024, 2048], P('fsdp', 'ctx')
- attn_gain_grad: float32 [2048], P(('fsdp', 'ctx'))
- query_grad: float32 [2048, 3072], P(('fsdp', 'ctx'), 'tp')
- latent_down_grad: float32 [2048, 576], P(('fsdp', 'ctx'))
- latent_gain_grad: float32 [512], P(('fsdp', 'ctx'))
- latent_up_grad: float32 [512, 4096], P(('fsdp', 'ctx'), 'tp')
- output_grad: float32 [2048, 2048], P('tp', ('fsdp', 'ctx'))
- ffn_gain_grad: float32 [2048], P(('fsdp', 'ctx'))
- shared_gate_up_grad: float32 [2048, 2, 2816], P(('fsdp', 'ctx'), None, 'tp')
- shared_down_grad: float32 [2816, 2048], P('tp', ('fsdp', 'ctx'))
- expert_gate_up_grad: float32 [2048, 16, 2, 1408], P(('fsdp', 'ctx'), None, None, 'tp')
- expert_down_grad: float32 [2048, 16, 1408], P(('fsdp', 'ctx'), None, 'tp')
The draws below stay inside these ranges and needn't reach their ends.
Inputs may be any that keep to these rules, and one draw needn't show every extreme that they name: `lengths`: in each group of 2 consecutive sequences, one has length 1024. `routes`: A position's 6 experts differ. In each sequence's aligned block of 256 positions no expert is named more than 128 times, and in some block one is named exactly 128 times.
All inputs are finite; a program needn't handle non-finite values.
Results may differ from the reference program's by a relative error of at most 0.024.
Values may be sent and summed in bfloat16 or wider, within the bound.
A program may use at most 512 MiB of HBM per device.

```python
import math
import jax
import jax.numpy as jnp
import numpy as np
from jax import lax

D = 2048
HEADS = 16
NOPE = 128
ROPE = 64
VDIM = 128
RANK = 512
FF = 1408
SHARED = 2816
TOP = 6
EXPERTS = 16
SEQ = 1024
SEQ_DEV = 2
SEQS = 4
BLOCK = 256
MOST = 128
UNIT_BLOCKS = 4
N_CTX = 4


def draw_lengths(key, part):
    key = jax.random.fold_in(key, 11)
    first_key, second_key = jax.random.split(key)
    drawn = jax.random.randint(first_key, (SEQS,), SEQ // 4, SEQ + 1, dtype=jnp.int32)
    picks = jax.random.randint(second_key, (SEQS // SEQ_DEV,), 0, SEQ_DEV, dtype=jnp.int32)
    grouped = drawn.reshape(SEQS // SEQ_DEV, SEQ_DEV)
    chosen = jnp.arange(SEQ_DEV, dtype=jnp.int32)[None, :] == picks[:, None]
    return jnp.where(chosen, SEQ, grouped).reshape(SEQS).astype(jnp.int32)


def block_scale(stream_key, shape, cuts, smallest, largest):
    level, own = 1.0, jax.random.fold_in(stream_key, 6)
    for position, parts in cuts:
        draws = jnp.exp(jax.random.uniform(jax.random.fold_in(own, position), (parts,), jnp.float32, smallest / len(cuts), largest / len(cuts)))
        level = level * jnp.repeat(draws, shape[position] // parts).reshape([-1 if axis == position else 1 for axis in range(len(shape))])
    return level


def deal_out(own_key, own, number, rows, count, top, most, lean):
    order = jax.random.permutation(own_key, count)
    packed, common = shares(count, rows * top, most, lean, True), shares(count, rows * top, most, lean, False)
    places = jnp.arange(count)

    def named(sizes, rotation):
        used = int((sizes > 0).sum())
        fixed = max(1, used // 4)
        passed = fixed + (places - fixed + rotation * (used - fixed)) % max(1, count - fixed)
        return jnp.zeros((count,), jnp.int32).at[order[jnp.where(places < fixed, places, passed)]].set(jnp.asarray(sizes, jnp.int32))

    sizes = jnp.where(number % 4 == 0, named(packed, number // 4), named(common, number - number // 4 - 1))
    mixed = jax.random.permutation(jax.random.fold_in(own, 3), count)
    giver, sink = mixed[0:count // 2 * 2:2], mixed[1:count // 2 * 2:2]
    slack = jnp.minimum(sizes[giver] - 1, most - sizes[sink]) // 2
    slack = jnp.where((giver == order[0]) | (sink == order[0]) | (sizes[sink] == 0), 0, jnp.maximum(slack, 0))
    passed = jax.random.randint(jax.random.fold_in(own, 4), (count // 2,), 0, 1 << 20) % (slack + 1)
    sizes = sizes.at[giver].add(-passed).at[sink].add(passed)
    labels = jnp.searchsorted(jnp.cumsum(sizes), jnp.arange(rows * top), side="right").astype(jnp.int32)
    grid = labels.reshape(top, rows).T
    grid = grid[jax.random.permutation(jax.random.fold_in(own, 1), rows)]
    rotation = jax.random.randint(jax.random.fold_in(own, 2), (rows, 1), 0, top)
    return jnp.take_along_axis(grid, (jnp.arange(top)[None, :] + rotation) % top, axis=1)


def shares(amount, total, reach, lean, full):
    loads = [(1 << 20) // math.isqrt(grade ** lean) + 1 for grade in range(1, amount + 1)]
    largest = reach if full else min(reach, max(-(-total // amount), total * loads[0] // sum(loads)))
    least = 1 if total - largest >= amount - 1 else 0
    given, spare = [largest] + [least] * (amount - 1), total - largest - least * (amount - 1)
    while spare > 0:
        movable = [i for i in range(1, amount) if given[i] < largest] or [i for i in range(1, amount) if given[i] < reach]
        mass, left = sum([loads[i] for i in movable]), spare
        for i in movable:
            addition = min(reach - given[i], max(1, left * loads[i] // mass), spare)
            given[i] = given[i] + addition
            spare = spare - addition
    return np.array(given)


def centred(key, dims, deviation, limit, cuts=(), kind=jnp.bfloat16):
    level = block_scale(key, dims, cuts, -0.22, 0.18) if cuts else 1.0
    array = jax.random.normal(key, dims, jnp.float32) * deviation * level
    return jnp.minimum(jnp.maximum(array, -limit), limit).astype(kind)


def setup_inputs(seed: int = 0) -> dict:
    keys = jax.random.split(jax.random.key(seed), 17)
    hidden_in = centred(keys[0], (SEQS, SEQ, D), 1.0, 6.0, ((0, 2), (1, 4)))
    lengths = draw_lengths(jax.random.fold_in(keys[16], 71), 0)
    routes_keys = jax.random.split(jax.random.fold_in(keys[2], 1), SEQS * SEQ // BLOCK)
    routes_turns = jax.random.permutation(jax.random.fold_in(keys[2], 3), SEQS * SEQ // BLOCK)
    routes = jax.vmap(lambda own, number: deal_out(jax.random.fold_in(keys[2], 2), own, number, BLOCK, EXPERTS, TOP, MOST, 2))(routes_keys, routes_turns).reshape((SEQS, SEQ, TOP))
    gate_weights = jnp.clip(jnp.exp(math.log(0.5) - 1.609438 * jax.random.uniform(keys[3], (SEQS, SEQ, TOP), jnp.float32) ** block_scale(keys[3], (SEQS, SEQ, TOP), ((0, 2), (1, 4)), -0.2, 0.2)), 0.1, 0.5)
    cotangent = centred(keys[4], (SEQS, SEQ, D), 1.0, 6.0, ((0, 2), (1, 4)))
    attn_gain = jnp.clip(1.0 + 0.1 * jax.random.normal(keys[5], (D,), jnp.float32), 0.5, 1.5).astype(jnp.bfloat16)
    query_weight = centred(keys[6], (D, HEADS * (NOPE + ROPE)), D ** -0.5, 0.125, ((0, 8), (1, 4)))
    latent_down = centred(keys[7], (D, RANK + ROPE), D ** -0.5, 0.125, ((0, 8),))
    latent_gain = jnp.clip(1.0 + 0.1 * jax.random.normal(keys[8], (RANK,), jnp.float32), 0.5, 1.5).astype(jnp.bfloat16)
    latent_up = centred(keys[9], (RANK, HEADS * (NOPE + VDIM)), RANK ** -0.5, 0.25, ((0, 8), (1, 4)))
    output_weight = centred(keys[10], (HEADS * VDIM, D), (HEADS * VDIM // 8) ** -0.5, 0.375, ((0, 4), (1, 8)))
    ffn_gain = jnp.clip(1.0 + 0.1 * jax.random.normal(keys[11], (D,), jnp.float32), 0.5, 1.5).astype(jnp.bfloat16)
    shared_gate_up = centred(keys[12], (D, 2, SHARED), D ** -0.5, 0.125, ((0, 8), (2, 4)))
    shared_down = centred(keys[13], (SHARED, D), SHARED ** -0.5, 0.109375, ((0, 4), (1, 8)))
    expert_gate_up = centred(keys[14], (D, EXPERTS, 2, FF), D ** -0.5, 0.125, ((0, 8), (3, 4)))
    expert_down = centred(keys[15], (D, EXPERTS, FF), FF ** -0.5, 0.15625, ((0, 8), (2, 4)))
    return {"hidden_in": hidden_in, "lengths": lengths, "routes": routes, "gate_weights": gate_weights, "cotangent": cotangent, "attn_gain": attn_gain, "query_weight": query_weight, "latent_down": latent_down, "latent_gain": latent_gain, "latent_up": latent_up, "output_weight": output_weight, "ffn_gain": ffn_gain, "shared_gate_up": shared_gate_up, "shared_down": shared_down, "expert_gate_up": expert_gate_up, "expert_down": expert_down}


@jax.custom_vjp
def low(v):
    return lax.optimization_barrier(v.astype(jnp.bfloat16)).astype(jnp.float32)

@jax.custom_vjp
def low_back(v):
    return v

def low_keep(v):
    return (low(v), None)

def low_pass(kept, grad):
    return (grad,)

def back_keep(v):
    return (v, None)

def back_low(kept, grad):
    return (low(grad),)
low.defvjp(low_keep, low_pass)
low_back.defvjp(back_keep, back_low)
HIGH = lax.Precision.HIGHEST
EPS = 1e-06

def rms_scale(values):
    return lax.rsqrt(lax.optimization_barrier(jnp.mean(values * values, axis=-1, keepdims=True)) + EPS)

def rotate(values, cosine, sine):
    half = values.shape[-1] // 2
    first = values[..., :half]
    second = values[..., half:]
    return jnp.concatenate([first * cosine - second * sine, first * sine + second * cosine], -1)

def layer(hidden, weights, length, routes, gate_weights):
    attn_gain, query_weight, latent_down, latent_gain, latent_up, output_weight, ffn_gain, shared_gate_up, shared_down, expert_gate_up, expert_down = weights
    inverse = 10000.0 ** (-jnp.arange(ROPE // 2, dtype=jnp.float32) / (ROPE // 2))
    angles = jnp.arange(SEQ, dtype=jnp.float32)[:, None] * inverse[None, :]
    cosine = jnp.cos(angles)
    sine = jnp.sin(angles)
    low_one = low(hidden * rms_scale(hidden) * attn_gain)
    query_pre = low_back(jnp.dot(low_one, query_weight, precision=HIGH)).reshape(SEQ, HEADS, NOPE + ROPE)
    queries = low(jnp.concatenate([query_pre[..., :NOPE], rotate(query_pre[..., NOPE:], cosine[:, None], sine[:, None])], -1))
    latent_pre = low_back(jnp.dot(low_one, latent_down, precision=HIGH))
    latent = latent_pre[:, :RANK]
    lat_keys = low(latent * rms_scale(latent) * latent_gain)
    rope_keys = low(rotate(latent_pre[:, RANK:], cosine, sine))
    key_pos = jnp.arange(SEQ, dtype=jnp.int32)
    scale = (NOPE + ROPE) ** (-0.5)

    def one_block(index):
        start = index * BLOCK
        block_queries = lax.dynamic_slice_in_dim(queries, start, BLOCK, 0)
        expanded = low(low_back(jnp.dot(lat_keys, latent_up, precision=HIGH))).reshape(SEQ, HEADS, NOPE + VDIM)
        full_keys = jnp.concatenate([expanded[..., :NOPE], jnp.broadcast_to(rope_keys[:, None, :], (SEQ, HEADS, ROPE))], -1)
        values = expanded[..., NOPE:]
        raw = low_back(jnp.einsum('ihd,jhd->hij', block_queries, full_keys, precision=HIGH) * scale)
        rows_at = start + jnp.arange(BLOCK, dtype=jnp.int32)
        keep = (key_pos[None, :] <= rows_at[:, None]) & (key_pos[None, :] < length)
        masked = jnp.where(keep[None], raw, -1e+30)
        peak = lax.optimization_barrier(jnp.max(masked, axis=-1, keepdims=True))
        expo = jnp.exp(masked - peak)
        probs = expo / lax.optimization_barrier(jnp.sum(expo, axis=-1, keepdims=True))
        return jnp.einsum('hij,jhd->ihd', low(probs), values, precision=HIGH)
    heads_out = lax.map(jax.checkpoint(one_block), jnp.arange(N_CTX, dtype=jnp.int32))
    attended = low(low_back(heads_out.reshape(SEQ, HEADS * VDIM)))
    middle = hidden + low_back(jnp.dot(attended, output_weight, precision=HIGH))
    low_two = low(middle * rms_scale(middle) * ffn_gain)
    shared_gu = low_back(jnp.dot(low_two, shared_gate_up.reshape(D, 2 * SHARED), precision=HIGH)).reshape(SEQ, 2, SHARED)
    shared_hidden = low(jax.nn.silu(shared_gu[:, 0]) * shared_gu[:, 1])
    shared_out = low_back(jnp.dot(shared_hidden, shared_down, precision=HIGH))
    capacity = N_CTX * MOST
    flat_routes = routes.reshape(-1)
    onehot = (flat_routes[:, None] == jnp.arange(EXPERTS, dtype=jnp.int32)[None, :]).astype(jnp.int32)
    ranks = lax.optimization_barrier(jnp.sum((jnp.cumsum(onehot, axis=0) - onehot) * onehot, axis=1))
    slots = (flat_routes * capacity + ranks).astype(jnp.int32)
    owners = jnp.zeros((EXPERTS * capacity,), jnp.int32).at[slots].set(jnp.arange(SEQ * TOP, dtype=jnp.int32) // TOP)
    filled = jnp.zeros((EXPERTS * capacity,), jnp.float32).at[slots].set(1.0)
    slot_inputs = (low_two[owners] * filled[:, None]).reshape(EXPERTS, capacity, D)
    block_width = FF // UNIT_BLOCKS
    block_inputs = low_back(jnp.broadcast_to(slot_inputs[None], (UNIT_BLOCKS, EXPERTS, capacity, D)))
    gate_up_blocks = expert_gate_up.reshape(D, EXPERTS, 2, UNIT_BLOCKS, block_width)
    expert_gu = low_back(jnp.einsum('qecd,degqf->ecgqf', block_inputs, gate_up_blocks, precision=HIGH)).reshape(EXPERTS, capacity, 2, FF)
    expert_hidden = low(jax.nn.silu(expert_gu[:, :, 0]) * expert_gu[:, :, 1])
    down_blocks = expert_down.reshape(D, EXPERTS, UNIT_BLOCKS, block_width)
    out_blocks = low(jnp.einsum('ecqf,deqf->ecqd', expert_hidden.reshape(EXPERTS, capacity, UNIT_BLOCKS, block_width), down_blocks, precision=HIGH))
    expert_out = low_back(lax.optimization_barrier(jnp.sum(out_blocks, axis=2)))
    picked = expert_out.reshape(EXPERTS * capacity, D)[slots].reshape(SEQ, TOP, D)
    routed = lax.optimization_barrier(jnp.sum(gate_weights[:, :, None] * picked, axis=1))
    return middle + shared_out + routed

def reference(hidden_in, lengths, routes, gate_weights, cotangent, attn_gain, query_weight, latent_down, latent_gain, latent_up, output_weight, ffn_gain, shared_gate_up, shared_down, expert_gate_up, expert_down):
    weights = tuple((w.astype(jnp.float32) for w in (attn_gain, query_weight, latent_down, latent_gain, latent_up, output_weight, ffn_gain, shared_gate_up, shared_down, expert_gate_up, expert_down)))

    def one_seq(carry, item):
        hidden, length, seq_routes, seq_gates, seq_cot = item

        def forward(values, params):
            return layer(values, params, length, seq_routes, seq_gates)
        out_value, pullback = jax.vjp(forward, hidden.astype(jnp.float32), weights)
        valid = (jnp.arange(SEQ, dtype=jnp.int32) < length).astype(jnp.float32)
        grad_in, grad_weights = pullback(seq_cot.astype(jnp.float32) * valid[:, None])
        carry = jax.tree.map(lambda acc, new: acc + new, carry, grad_weights)
        return (carry, (out_value.astype(jnp.bfloat16), grad_in))
    start = tuple((jnp.zeros_like(w) for w in weights))
    sums, (outputs, grads_in) = lax.scan(one_seq, start, (hidden_in, lengths, routes, gate_weights, cotangent))
    return (outputs, grads_in, sums[0], sums[1], sums[2], sums[3], sums[4], sums[5], sums[6], sums[7], sums[8], sums[9], sums[10])
```

```python
import functools

import jax
import jax.numpy as jnp
from jax import lax
from jax.experimental import pallas as pl
from jax.experimental.pallas import tpu as pltpu
from jax.sharding import PartitionSpec as P

NOPE = 128
ROPE = 64
VDIM = 128
RANK = 512
TOP = 6
EXPERTS = 16
EPS = 1e-06
PLANE = ("fsdp", "ctx")
BF = jnp.bfloat16
F32 = jnp.float32


def rms_scale(values):
    return lax.rsqrt(jnp.mean(values * values, axis=-1, keepdims=True) + EPS)


def rotate(values, cosine, sine):
    half = values.shape[-1] // 2
    first = values[..., :half]
    second = values[..., half:]
    return jnp.concatenate([first * cosine - second * sine, first * sine + second * cosine], -1)


def rotate_back(grads, cosine, sine):
    half = grads.shape[-1] // 2
    first = grads[..., :half]
    second = grads[..., half:]
    return jnp.concatenate([first * cosine + second * sine, second * cosine - first * sine], -1)


def norm_back(values, scale, gain, grads):
    weighted = gain * grads
    return scale * weighted - values * (scale * scale * scale) * jnp.mean(
        weighted * values, axis=-1, keepdims=True
    )


def silu_parts(pre):
    sigma = jax.nn.sigmoid(pre)
    return (pre * sigma, sigma * (1.0 + pre * (1.0 - sigma)))


def dot(spec, a, b):
    return jnp.einsum(spec, a, b, preferred_element_type=F32)


def chip_shift(value, folds, chips_x, df, dx):
    if df == 0 and dx == 0:
        return value
    width = 2 * chips_x
    pairs = []
    for f in range(folds):
        for x in range(chips_x):
            for core in range(2):
                pairs.append(
                    (
                        f * width + 2 * x + core,
                        ((f + df) % folds) * width + 2 * ((x + dx) % chips_x) + core,
                    )
                )
    return lax.ppermute(value, PLANE, pairs)


def core_swap(value, folds, chips_x):
    count = folds * 2 * chips_x
    return lax.ppermute(value, PLANE, [(i, i ^ 1) for i in range(count)])


def first_hops(value, folds, chips_x, along=None):
    got = {}
    for df in range(folds):
        for dx in range(chips_x):
            if along is not None and dx == 0:
                got[df, dx] = along[df]
            elif df == 0 or dx == 0:
                got[df, dx] = chip_shift(value, folds, chips_x, df, dx)
    return got


def second_hops(got, folds, chips_x):
    half = got[0, 0].shape[-1] // 2
    for df in range(1, folds):
        for dx in range(1, chips_x):
            got[df, dx] = jnp.concatenate(
                [
                    chip_shift(got[0, dx][..., :half], folds, chips_x, df, 0),
                    chip_shift(got[df, 0][..., half:], folds, chips_x, 0, dx),
                ],
                -1,
            )
    return [got[df, dx] for df in range(folds) for dx in range(chips_x)]

def pieces_for(value, folds, chips_x):
    fold_at, ctx_at = lax.axis_index("fsdp"), lax.axis_index("ctx")
    for df in range(folds):
        for dx in range(chips_x):
            to = ((fold_at + df) % folds) * chips_x + (ctx_at // 2 + dx) % chips_x
            yield lax.dynamic_index_in_dim(value, to, 0, False), df, dx


def row_gather(value, folds, chips_x):
    got = jnp.stack([chip_shift(value, folds, chips_x, 0, dx) for dx in range(chips_x)])
    return jnp.concatenate([got, core_swap(got, folds, chips_x)])


def row_reduce(parts, folds, chips_x):
    both = parts[:chips_x].astype(F32) + core_swap(parts[chips_x:], folds, chips_x).astype(F32)
    total = both[0]
    for dx in range(1, chips_x):
        total = total + chip_shift(both[dx].astype(BF), folds, chips_x, 0, -dx).astype(F32)
    return total


def plane_reduce(parts, folds, chips_x):
    chips = folds * chips_x
    both = parts[:chips].astype(F32) + core_swap(parts[chips:], folds, chips_x).astype(F32)
    both = both.astype(BF)
    total = None
    for df in range(folds):
        for dx in range(chips_x):
            one = chip_shift(both[df * chips_x + dx], folds, chips_x, -df, -dx).astype(F32)
            total = one if total is None else total + one
    return total


def dot_nn(a, b):
    return lax.dot_general(a, b, (((1,), (0,)), ((), ())), preferred_element_type=F32)


def dot_nt(a, b):
    return lax.dot_general(a, b, (((1,), (1,)), ((), ())), preferred_element_type=F32)


def dot_tn(a, b):
    return lax.dot_general(a, b, (((0,), (0,)), ((), ())), preferred_element_type=F32)


class Sizes:
    def __init__(self, chips, per_chip, units, part, seqs, block, width):
        self.chips, self.per_chip, self.units, self.part = chips, per_chip, units, part
        self.seqs, self.block, self.width = seqs, block, width
        self.tokens = seqs * block
        self.capacity = block // 2
        self.slots = seqs * self.capacity
        self.row_a = per_chip * 2 * units
        self.row_b = self.row_a + per_chip * units
        self.row_c = self.row_b + 2 * part
        self.rows = self.row_c + part


def placement(sizes, code_ref, at):
    span = pl.ds(at * sizes.block, sizes.block)
    index = lax.broadcasted_iota(jnp.int32, (sizes.capacity, sizes.block), 0).astype(F32)
    rows = [
        jnp.where(code_ref[e : e + 1, span] == index, 1.0, 0.0) for e in range(sizes.per_chip)
    ]
    return jnp.concatenate(rows, 0)


def slot_gates(sizes, place, gate_ref, at):
    span = pl.ds(at * sizes.block, sizes.block)
    cap = sizes.capacity
    columns = [
        jnp.sum(place[e * cap : (e + 1) * cap] * gate_ref[e : e + 1, span], -1, keepdims=True)
        for e in range(sizes.per_chip)
    ]
    return jnp.concatenate(columns, 0)


def chunk_kernel(sizes, straight, *refs):
    code_ref, gate_ref, x_ref, g_ref = refs[:4]
    count = 2 * sizes.chips if straight else 1
    weight_refs, refs = refs[4 : 4 + count], refs[-9:]
    (in_ref, out_ref, acts_ref, shared_ref, w_ref, xs_ref, gs_ref, gate_cols, sems) = refs
    units, part, cap = sizes.units, sizes.part, sizes.capacity
    copies = []
    if straight:
        piece = weight_refs[0].shape[1]
        fold_at, ctx_at = lax.axis_index("fsdp"), lax.axis_index("ctx")
        folds, chips_x = lax.axis_size("fsdp"), lax.axis_size("ctx") // 2
        core = lax.rem(ctx_at, 2)
        for j, source in enumerate(weight_refs):
            df, dx = j % sizes.chips // chips_x, j % chips_x
            chip = lax.rem(fold_at + folds - df, folds) * chips_x + lax.rem(
                ctx_at // 2 + chips_x - dx, chips_x
            )
            side = core if j < sizes.chips else 1 - core
            column = pl.multiple_of((2 * chip + side) * piece, piece)
            copies.append(
                pltpu.make_async_copy(source, w_ref.at[:, pl.ds(column, piece)], sems.at[j])
            )
    else:
        copies.append(pltpu.make_async_copy(weight_refs[0], w_ref, sems.at[0]))
    for copy in copies:
        copy.start()
    for at in range(sizes.seqs):
        place = placement(sizes, code_ref, at)
        gates = slot_gates(sizes, place, gate_ref, at)
        place = place.astype(BF)
        span = pl.ds(at * sizes.block, sizes.block)
        rows_in = dot_nn(place, x_ref[span, :]).astype(BF)
        rows_grad = (dot_nn(place, g_ref[span, :]) * gates).astype(BF)
        for e in range(sizes.per_chip):
            xs_ref[e, at] = rows_in[e * cap : (e + 1) * cap]
            gs_ref[e, at] = rows_grad[e * cap : (e + 1) * cap]
            gate_cols[e, at] = jnp.broadcast_to(
                gates[e * cap : (e + 1) * cap], gate_cols.shape[2:]
            )
    for copy in copies:
        copy.wait()

    def one_expert(e):
        top, low = e * 2 * units, e * units
        gate_up = w_ref[pl.ds(top, 2 * units), :]
        down = w_ref[pl.ds(sizes.row_a + low, units), :]
        rows_in = xs_ref[e].reshape(sizes.slots, sizes.width)
        rows_grad = gs_ref[e].reshape(sizes.slots, sizes.width)
        pre = dot_nt(gate_up, rows_in)
        d_hidden = dot_nt(down, rows_grad)
        act, slope = silu_parts(pre[:units])
        up = pre[units:]
        hidden = (act * up).astype(BF)
        d_gu = jnp.concatenate([d_hidden * up * slope, d_hidden * act], 0).astype(BF)
        acts_ref[pl.ds(top, 2 * units), :] = d_gu
        acts_ref[pl.ds(sizes.row_a + low, units), :] = hidden
        back = dot_tn(d_gu, gate_up).astype(BF)
        xs_ref[e] = back.reshape(sizes.seqs, cap, sizes.width)
        gates = gate_cols[e].reshape(sizes.slots, gate_cols.shape[3])[:, :1]
        ahead = (dot_tn(hidden, down) * gates).astype(BF)
        gs_ref[e] = ahead.reshape(sizes.seqs, cap, sizes.width)

    for e in range(sizes.per_chip):
        one_expert(e)
    s_gate_up = w_ref[sizes.row_b : sizes.row_c, :]
    s_down = w_ref[sizes.row_c :, :]
    for at in range(sizes.seqs):
        span = pl.ds(at * sizes.block, sizes.block)
        pre = dot_nt(s_gate_up, x_ref[span, :])
        d_hidden = dot_nt(s_down, g_ref[span, :])
        act, slope = silu_parts(pre[:part])
        up = pre[part:]
        hidden = (act * up).astype(BF)
        d_gu = jnp.concatenate([d_hidden * up * slope, d_hidden * act], 0).astype(BF)
        shared_ref[: 2 * part, span] = d_gu
        shared_ref[2 * part :, span] = hidden
        place = placement(sizes, code_ref, at).astype(BF)
        back = jnp.concatenate([xs_ref[e, at] for e in range(sizes.per_chip)], 0)
        in_ref[span, :] = (dot_tn(place, back) + dot_tn(d_gu, s_gate_up)).astype(BF)
        ahead = jnp.concatenate([gs_ref[e, at] for e in range(sizes.per_chip)], 0)
        out_ref[span, :] = (dot_tn(place, ahead) + dot_tn(hidden, s_down)).astype(BF)


def chunk_call(sizes, number, weights, code, gate, x_rows, g_rows, saved):
    straight = len(weights) > 1
    whole = lambda shape: pl.BlockSpec(shape, lambda i: (0,) * len(shape), pipeline_mode=pl.Buffered(1))
    anywhere = pl.BlockSpec(memory_space=pl.ANY)
    rows = (sizes.tokens, sizes.width)
    first = 4 + len(weights)
    saved = [] if saved is None else list(saved)
    acts_shape = (sizes.row_b, sizes.chips * sizes.slots)
    shared_shape = (3 * sizes.part, sizes.chips * sizes.tokens)
    flops = 2 * sizes.width * (
        6 * sizes.per_chip * 2 * sizes.units * sizes.slots // 2
        + 6 * sizes.part * sizes.tokens
        + 4 * sizes.per_chip * sizes.slots * sizes.block
    )
    return pl.pallas_call(
        functools.partial(chunk_kernel, sizes, straight),
        grid=(1,),
        in_specs=[whole(code.shape), whole(gate.shape), whole(rows), whole(rows)]
        + [anywhere] * (len(weights) + len(saved)),
        out_specs=[
            whole(rows),
            whole(rows),
            pl.BlockSpec((acts_shape[0], sizes.slots), lambda i: (0, number)),
            pl.BlockSpec((shared_shape[0], sizes.tokens), lambda i: (0, number)),
        ],
        out_shape=[
            jax.ShapeDtypeStruct(rows, BF),
            jax.ShapeDtypeStruct(rows, BF),
            jax.ShapeDtypeStruct(acts_shape, BF),
            jax.ShapeDtypeStruct(shared_shape, BF),
        ],
        scratch_shapes=[
            pltpu.VMEM((sizes.rows, sizes.width), BF),
            pltpu.VMEM((sizes.per_chip, sizes.seqs, sizes.capacity, sizes.width), BF),
            pltpu.VMEM((sizes.per_chip, sizes.seqs, sizes.capacity, sizes.width), BF),
            pltpu.VMEM((sizes.per_chip, sizes.seqs, sizes.capacity, 128), F32),
            pltpu.SemaphoreType.DMA((2 * sizes.chips,)),
        ],
        input_output_aliases={first: 2, first + 1: 3} if saved else {},
        compiler_params=pltpu.CompilerParams(vmem_limit_bytes=60 * 1024 * 1024),
        cost_estimate=pl.CostEstimate(
            flops=flops, bytes_accessed=2 * sizes.rows * sizes.width, transcendentals=0
        ),
        name="expert_rows",
    )(code, gate, x_rows, g_rows, *weights, *saved)


def weight_grad_kernel(sizes, straight, *refs):
    count = sizes.chips
    code_ref, gate_ref, acts_ref, shared_ref = refs[:4]
    x_refs, g_refs = refs[4 : 4 + count], refs[4 + count : 4 + 2 * count]
    outs = refs[4 + 2 * count : -2]
    xs_ref, gs_ref = refs[-2:]
    units, part, cap = sizes.units, sizes.part, sizes.capacity
    core = lax.rem(lax.axis_index("ctx"), 2)

    def put(start, size, grad):
        if not straight:
            outs[0][pl.ds(start, size), :] = grad.astype(BF)
            return
        half = grad.shape[1] // 2
        low, high = grad[:, :half].astype(BF), grad[:, half:].astype(BF)
        outs[0][0, pl.ds(start, size), :] = jnp.where(core == 0, low, high)
        outs[1][0, pl.ds(start, size), :] = jnp.where(core == 0, high, low)

    for c in range(count):
        for at in range(sizes.seqs):
            place = placement(sizes, code_ref.at[c], at)
            gates = slot_gates(sizes, place, gate_ref.at[c], at)
            place = place.astype(BF)
            span = pl.ds(at * sizes.block, sizes.block)
            rows_in = dot_nn(place, x_refs[c][span, :]).astype(BF)
            rows_grad = (dot_nn(place, g_refs[c][span, :]) * gates).astype(BF)
            into = pl.ds(c * sizes.slots + at * cap, cap)
            for e in range(sizes.per_chip):
                xs_ref[e, into] = rows_in[e * cap : (e + 1) * cap]
                gs_ref[e, into] = rows_grad[e * cap : (e + 1) * cap]

    def one_expert(e):
        top, low = e * 2 * units, e * units
        put(top, 2 * units, dot_nn(acts_ref[pl.ds(top, 2 * units), :], xs_ref[e]))
        put(
            sizes.row_a + low,
            units,
            dot_nn(acts_ref[pl.ds(sizes.row_a + low, units), :], gs_ref[e]),
        )

    for e in range(sizes.per_chip):
        one_expert(e)
    d_gu_sum, down_sum = None, None
    for c in range(count):
        span = pl.ds(c * sizes.tokens, sizes.tokens)
        one = dot_nn(shared_ref[: 2 * part, span], x_refs[c][...])
        two = dot_nn(shared_ref[2 * part :, span], g_refs[c][...])
        d_gu_sum = one if d_gu_sum is None else d_gu_sum + one
        down_sum = two if down_sum is None else down_sum + two
    put(sizes.row_b, 2 * part, d_gu_sum)
    put(sizes.row_c, part, down_sum)


def weight_grad_call(sizes, rows_local, code, gate, acts, shared_acts, x_chunks, g_chunks):
    straight = rows_local % 128 == 0
    columns = 2 * rows_local if straight else 256
    steps = sizes.width // columns
    whole = lambda shape: pl.BlockSpec(shape, lambda j: (0,) * len(shape), pipeline_mode=pl.Buffered(1))
    cols = pl.BlockSpec((sizes.tokens, columns), lambda j: (0, j))
    if straight:
        out_specs = [pl.BlockSpec((1, sizes.rows, rows_local), lambda j: (j, 0, 0))] * 2
        out_shape = [jax.ShapeDtypeStruct((sizes.chips, sizes.rows, rows_local), BF)] * 2
    else:
        out_specs = [pl.BlockSpec((sizes.rows, columns), lambda j: (0, j))]
        out_shape = [jax.ShapeDtypeStruct((sizes.rows, sizes.width), BF)]
    slots = sizes.chips * sizes.slots
    flops = 2 * sizes.width * (
        3 * sizes.per_chip * sizes.units * slots
        + 3 * sizes.part * sizes.tokens * sizes.chips
        + 2 * sizes.per_chip * slots * sizes.block
    )
    return pl.pallas_call(
        functools.partial(weight_grad_kernel, sizes, straight),
        grid=(steps,),
        in_specs=[whole(code.shape), whole(gate.shape), whole(acts.shape), whole(shared_acts.shape)]
        + [cols] * (2 * sizes.chips),
        out_specs=out_specs,
        out_shape=out_shape,
        scratch_shapes=[
            pltpu.VMEM((sizes.per_chip, slots, columns), BF),
            pltpu.VMEM((sizes.per_chip, slots, columns), BF),
        ],
        compiler_params=pltpu.CompilerParams(vmem_limit_bytes=60 * 1024 * 1024),
        cost_estimate=pl.CostEstimate(
            flops=flops, bytes_accessed=4 * sizes.rows * sizes.width, transcendentals=0
        ),
        name="expert_weight_grads",
    )(code, gate, acts, shared_acts, *x_chunks, *g_chunks)


def block_columns(count, piece):
    if count == 1:
        return [0]
    fold_at, ctx_at = lax.axis_index("fsdp"), lax.axis_index("ctx")
    folds, chips_x = lax.axis_size("fsdp"), lax.axis_size("ctx") // 2
    core = lax.rem(ctx_at, 2)
    columns = []
    for side in (core, 1 - core):
        for df in range(folds):
            for dx in range(chips_x):
                chip = lax.rem(fold_at + folds - df, folds) * chips_x + lax.rem(
                    ctx_at // 2 + chips_x - dx, chips_x
                )
                columns.append(pl.multiple_of((2 * chip + side) * piece, piece))
    return columns


class Rows:
    def __init__(self, out_rows, query_cols, up_rows, info_rows):
        self.heads = out_rows // VDIM
        self.out = out_rows
        self.nope = out_rows + self.heads * NOPE
        self.query = out_rows + query_cols
        self.latent = self.query + RANK
        self.rope = self.latent + ROPE
        self.up = self.rope + up_rows
        self.info = self.up + info_rows
        self.total = self.info + 16


def lanes_of(shape):
    return lax.broadcasted_iota(jnp.int32, shape, 1)


def spread(mixed):
    turned = pltpu.roll(mixed, ROPE // 2, 1)
    even = lax.rem(lanes_of(mixed.shape) // (ROPE // 2), 2) == 0
    return jnp.where(even, mixed, turned), jnp.where(even, turned, mixed)


def mix(first, second):
    even = lax.rem(lanes_of(first.shape) // (ROPE // 2), 2) == 0
    return jnp.where(even, first, second)


def project_kernel(rows, count, hidden_ref, gain_ref, cos_ref, sin_ref, *refs):
    blocks = refs[:count]
    low_ref, nope_ref, rope_ref, keys_ref, latent_ref, q_ref, kr_ref, x_ref = refs[count:]
    piece = blocks[0].shape[1]
    x = hidden_ref[...].astype(F32)
    x_ref[...] = x * rms_scale(x)
    for j, column in enumerate(block_columns(count, piece)):
        span = pl.ds(column, piece)
        block = blocks[j]
        low = (x_ref[:, span] * block[rows.info : rows.info + 1, :].astype(F32)).astype(BF)
        low_ref[:, span] = low
        half = ROPE // 2
        first = block[rows.latent : rows.latent + half, :]
        second = block[rows.latent + half : rows.rope, :]
        query = dot_nt(low, block[rows.out : rows.query, :])
        latent = dot_nt(low, block[rows.query : rows.latent, :])
        rope = dot_nt(low, jnp.concatenate([first] * 4 + [second] * 4, 0))
        if j == 0:
            q_ref[...], latent_ref[...], kr_ref[...] = query, latent, rope
        else:
            q_ref[...] += query
            latent_ref[...] += latent
            kr_ref[...] += rope
    cosine, sine = cos_ref[...], sin_ref[...]
    wide = rows.nope - rows.out
    side = (rows.query - rows.nope) // 2
    nope_ref[...] = q_ref[:, :wide].astype(BF)
    first, second = q_ref[:, wide : wide + side], q_ref[:, wide + side :]
    rope_ref[:, :side] = (first * cosine - second * sine).astype(BF)
    rope_ref[:, side:] = (first * sine + second * cosine).astype(BF)
    first, second = kr_ref[:, :128], kr_ref[:, 128:]
    latent = latent_ref[...]
    keys_ref[:, :RANK] = (latent * rms_scale(latent) * gain_ref[...]).astype(BF)
    keys_ref[:, RANK:] = mix(first * cosine - second * sine, first * sine + second * cosine).astype(BF)


def whole_spec(shape, rows=None):
    if rows is not None:
        shape = (rows,) + tuple(shape[1:])
    return pl.BlockSpec(
        tuple(shape), lambda i: (0,) * len(shape), pipeline_mode=pl.Buffered(1)
    )


def one_step(body, name, inputs, outputs, scratch, flops, scalars=()):
    arrays = [item[0] if isinstance(item, tuple) else item for item in inputs]
    specs = [
        whole_spec(item[0].shape, item[1]) if isinstance(item, tuple) else whole_spec(item.shape)
        for item in inputs
    ]
    smem = [pl.BlockSpec(memory_space=pltpu.SMEM)] * len(scalars)
    return pl.pallas_call(
        body,
        grid=(1,),
        in_specs=smem + specs,
        out_specs=[whole_spec(shape) for shape, _ in outputs],
        out_shape=[jax.ShapeDtypeStruct(shape, kind) for shape, kind in outputs],
        scratch_shapes=scratch,
        compiler_params=pltpu.CompilerParams(vmem_limit_bytes=60 * 1024 * 1024),
        cost_estimate=pl.CostEstimate(flops=flops, bytes_accessed=8 << 20, transcendentals=0),
        name=name,
    )(*scalars, *arrays)


def head_mask(shape, h):
    return lax.rem(lanes_of(shape) // (ROPE // 2), 128 // (ROPE // 2)) == h


def key_mask(lengths_ref, s, block, n_ctx):
    ctx_at = lax.axis_index("ctx")
    chips_x = n_ctx // 2
    core = lax.rem(ctx_at, 2)
    at = ctx_at * block + lax.broadcasted_iota(jnp.int32, (block, block), 0)
    within = lax.broadcasted_iota(jnp.int32, (block, block), 1)
    parts = []
    for side in (core, 1 - core):
        for dx in range(chips_x):
            start = (2 * lax.rem(ctx_at // 2 + chips_x - dx, chips_x) + side) * block
            key = start + within
            parts.append((key <= at) & (key < lengths_ref[s]))
    return jnp.concatenate([jnp.where(part, 0.0, -1e30) for part in parts], 1)


def attend_kernel(rows, count, seqs, block, n_ctx, lengths_ref, nope_ref, rope_ref, keys_ref, up_ref, *refs):
    blocks = refs[:count]
    part_ref, att_ref, exp_ref, lse_ref, kr_ref = refs[count:]
    piece = blocks[0].shape[1]
    scale = float(NOPE + ROPE) ** (-0.5)
    for s in range(seqs):
        here = pl.ds(s * block, block)
        for j in range(n_ctx):
            at = pl.ds(j * block, block)
            exp_ref[s, at, :] = dot_nn(keys_ref[j, s, :, :RANK], up_ref[...]).astype(BF)
            first, second = spread(keys_ref[j, s, :, RANK:].astype(F32))
            kr_ref[at, :128] = first.astype(BF)
            kr_ref[at, 128:] = second.astype(BF)
        bias = key_mask(lengths_ref, s, block, n_ctx)
        lse = jnp.zeros((block, 128), F32)
        for h in range(rows.heads):
            k = exp_ref[s, :, h * (NOPE + VDIM) : h * (NOPE + VDIM) + NOPE]
            v = exp_ref[s, :, h * (NOPE + VDIM) + NOPE : (h + 1) * (NOPE + VDIM)]
            q = nope_ref[here, h * NOPE : (h + 1) * NOPE]
            qr = rope_ref[here, :]
            qr = jnp.where(head_mask(qr.shape, h), qr, jnp.zeros_like(qr))
            raw = (dot_nt(q, k) + dot_nt(qr, kr_ref[...])) * scale
            masked = jnp.where(bias < 0.0, bias, raw)
            peak = jnp.max(masked, axis=-1, keepdims=True)
            expo = jnp.exp(masked - peak)
            total = jnp.sum(expo, axis=-1, keepdims=True)
            probs = (expo / total).astype(BF)
            att_ref[here, h * VDIM : (h + 1) * VDIM] = dot_nn(probs, v).astype(BF)
            lse = jnp.where(lanes_of(lse.shape) == h, peak + jnp.log(total), lse)
        lse_ref[here, :] = lse
    for j, column in enumerate(block_columns(count, piece)):
        part_ref[:, pl.ds(column, piece)] = dot_nn(att_ref[...], blocks[j][: rows.out, :]).astype(BF)


def attend_back_kernel(rows, count, seqs, block, n_ctx, lengths_ref, branch_ref, nope_ref, rope_ref,
                       keys_ref, exp_ref, lse_ref, up_ref, cos_ref, sin_ref, *refs):
    blocks = refs[:count]
    dq_ref, din_ref, dkeys_ref, up_grad_ref, datt_ref, dexp_ref, kr_ref, dkr_ref, sum_ref = refs[count:]
    piece = blocks[0].shape[1]
    scale = float(NOPE + ROPE) ** (-0.5)
    columns = block_columns(count, piece)
    side = (rows.query - rows.nope) // 2
    wide = rows.nope - rows.out
    for j, column in enumerate(columns):
        one = dot_nt(branch_ref[:, pl.ds(column, piece)], blocks[j][: rows.out, :])
        if j == 0:
            sum_ref[...] = one
        else:
            sum_ref[...] += one
    datt_ref[...] = sum_ref[...].astype(BF)
    for s in range(seqs):
        here = pl.ds(s * block, block)
        for j in range(n_ctx):
            at = pl.ds(j * block, block)
            first, second = spread(keys_ref[j, s, :, RANK:].astype(F32))
            kr_ref[at, :128] = first.astype(BF)
            kr_ref[at, 128:] = second.astype(BF)
        bias = key_mask(lengths_ref, s, block, n_ctx)
        lse_all = lse_ref[here, :]
        dq_rope = jnp.zeros((block, 2 * side), F32)
        for h in range(rows.heads):
            low, high = h * (NOPE + VDIM), (h + 1) * (NOPE + VDIM)
            k = exp_ref[s, :, low : low + NOPE]
            v = exp_ref[s, :, low + NOPE : high]
            q = nope_ref[here, h * NOPE : (h + 1) * NOPE]
            qr = rope_ref[here, :]
            mine = head_mask(qr.shape, h)
            qr = jnp.where(mine, qr, jnp.zeros_like(qr))
            datt = datt_ref[here, h * VDIM : (h + 1) * VDIM]
            raw = (dot_nt(q, k) + dot_nt(qr, kr_ref[...])) * scale
            lse = jnp.sum(jnp.where(lanes_of(lse_all.shape) == h, lse_all, 0.0), -1, keepdims=True)
            probs = jnp.exp(jnp.where(bias < 0.0, bias, raw) - lse)
            d_probs = dot_nt(datt, v)
            d_scores = probs * (d_probs - jnp.sum(probs * d_probs, axis=-1, keepdims=True))
            d_scores = d_scores.astype(BF)
            dq_ref[here, h * NOPE : (h + 1) * NOPE] = (dot_nn(d_scores, k) * scale).astype(BF)
            dq_rope = dq_rope + jnp.where(mine, dot_nn(d_scores, kr_ref[...]), 0.0)
            dexp_ref[:, low : low + NOPE] = (dot_tn(d_scores, q) * scale).astype(BF)
            dexp_ref[:, low + NOPE : high] = dot_tn(probs.astype(BF), datt).astype(BF)
            one = dot_tn(d_scores, qr)
            if h == 0:
                dkr_ref[...] = one
            else:
                dkr_ref[...] += one
        cosine, sine = cos_ref[here, :], sin_ref[here, :]
        first, second = dq_rope[:, :side] * scale, dq_rope[:, side:] * scale
        dq_ref[here, wide : wide + side] = (first * cosine + second * sine).astype(BF)
        dq_ref[here, wide + side :] = (second * cosine - first * sine).astype(BF)
        for j in range(n_ctx):
            at = pl.ds(j * block, block)
            folded = []
            for part in (dkr_ref[at, :128], dkr_ref[at, 128:]):
                part = part + pltpu.roll(part, 64, 1)
                folded.append((part + pltpu.roll(part, 32, 1)) * scale)
            dkeys_ref[j, s, :, RANK:] = mix(folded[0], folded[1]).astype(BF)
            dkeys_ref[j, s, :, :RANK] = dot_nt(dexp_ref[at, :], up_ref[...]).astype(BF)
            one = dot_tn(keys_ref[j, s, :, :RANK], dexp_ref[at, :])
            if s == 0 and j == 0:
                up_grad_ref[...] = one
            else:
                up_grad_ref[...] += one
    for j, column in enumerate(columns):
        din_ref[:, pl.ds(column, piece)] = dot_nn(dq_ref[...], blocks[j][rows.out : rows.query, :]).astype(BF)


def attend_grads_kernel(rows, count, piece, att_ref, branch_ref, dq_ref, low_ref, out_ref):
    for j, column in enumerate(block_columns(count, piece)):
        span = pl.ds(column, piece)
        out_ref[j, : rows.out, :] = dot_tn(att_ref[...], branch_ref[:, span]).astype(BF)
        out_ref[j, rows.out :, :] = dot_tn(dq_ref[...], low_ref[:, span]).astype(BF)


def last_kernel(rows, count, hidden_ref, low_ref, dq_ref, dlat_ref, dmid_ref, *refs):
    blocks = refs[:count]
    grad_ref, packed_ref, dlow_ref = refs[count:]
    piece = blocks[0].shape[1]
    columns = block_columns(count, piece)
    x = hidden_ref[...].astype(F32)
    scale = rms_scale(x)
    d_rope = dlat_ref[:, RANK:]
    d_rope = jnp.where(lanes_of(d_rope.shape) < ROPE, d_rope, jnp.zeros_like(d_rope))
    mean = jnp.zeros_like(scale)
    extra = packed_ref.shape[1] - (RANK + ROPE)
    for j, column in enumerate(columns):
        span = pl.ds(column, piece)
        block = blocks[j]
        d_low = dq_ref[:, span].astype(F32) + dot_nn(dlat_ref[:, :RANK], block[rows.query : rows.latent, :])
        d_low = d_low + dot_nn(d_rope, block[rows.latent : rows.latent + 128, :])
        x_part = hidden_ref[:, span].astype(F32)
        weighted = d_low * block[rows.info : rows.info + 1, :].astype(F32)
        dlow_ref[:, span] = weighted
        mean = mean + jnp.sum(weighted * x_part, axis=-1, keepdims=True)
        gain_grad = jnp.sum(d_low * x_part * scale, axis=0, keepdims=True)
        top = lax.broadcasted_iota(jnp.int32, (extra, piece), 0) == 0
        packed_ref[j, RANK + ROPE :, :] = jnp.where(top, gain_grad, 0.0).astype(BF)
        packed_ref[j, : RANK + ROPE, :] = dot_tn(dlat_ref[...], low_ref[:, span])[: RANK + ROPE].astype(BF)
    mean = mean * (scale * scale * scale) / hidden_ref.shape[1]
    grad_ref[...] = dmid_ref[...] + scale * dlow_ref[...] - hidden_ref[...].astype(F32) * mean


def local(
    hidden_in,
    lengths,
    routes,
    gate_weights,
    cotangent,
    attn_gain,
    query_weight,
    latent_down,
    latent_gain,
    latent_up,
    output_weight,
    ffn_gain,
    shared_gate_up,
    shared_down,
    expert_gate_up,
    expert_down,
):
    seq_dev, block, width = hidden_in.shape
    tokens = seq_dev * block
    folds, n_ctx = lax.axis_size("fsdp"), lax.axis_size("ctx")
    chips_x = n_ctx // 2
    chips = folds * chips_x
    plane = folds * n_ctx
    rows_local = expert_gate_up.shape[0]
    units = expert_gate_up.shape[-1]
    shared_units = shared_down.shape[0]
    per_chip = EXPERTS // chips
    shared_part = shared_units // chips
    fold_at, ctx_at = lax.axis_index("fsdp"), lax.axis_index("ctx")
    core = ctx_at % 2
    chip_at = fold_at * chips_x + ctx_at // 2
    same_core = [
        [(f * n_ctx + 2 * x + k) for f in range(folds) for x in range(chips_x)] for k in range(2)
    ]

    positions = ctx_at * block + jnp.arange(block, dtype=jnp.int32)
    valid = (positions[None, :] < lengths[:, None]).astype(F32)
    grad_out = cotangent.astype(F32) * valid[:, :, None]
    grad_low = grad_out.astype(BF)

    sizes = Sizes(
        chips, per_chip, units, shared_part + -shared_part % 16, seq_dev, block, width
    )
    experts_t = expert_gate_up.transpose(1, 2, 3, 0).reshape(chips, sizes.row_a, rows_local)
    edown_t = expert_down.transpose(1, 2, 0).reshape(chips, sizes.row_b - sizes.row_a, rows_local)
    extra = ((0, 0), (0, 0), (0, sizes.part - shared_part), (0, 0))
    shared_t = (
        shared_gate_up.transpose(1, 2, 0)
        .reshape(2, chips, shared_part, rows_local)
        .transpose(1, 0, 2, 3)
    )
    shared_t = jnp.pad(shared_t, extra).reshape(chips, 2 * sizes.part, rows_local)
    sdown_t = jnp.pad(shared_down.reshape(chips, 1, shared_part, rows_local), extra)
    sdown_t = sdown_t.reshape(chips, sizes.part, rows_local)
    to_chips = jnp.concatenate([experts_t, edown_t, shared_t, sdown_t], 1)
    named = routes[..., None] == jnp.arange(EXPERTS, dtype=jnp.int32)
    mask = jnp.any(named, axis=2)
    gate_of = jnp.sum(jnp.where(named, gate_weights[..., None], 0.0), axis=2)
    earlier = (jnp.arange(block)[:, None] > jnp.arange(block)[None, :]).astype(BF)
    ranks = dot("ut,ste->sue", earlier, mask.astype(BF))
    code = jnp.where(mask, ranks, -1.0)
    gate_high = lax.reduce_precision(gate_of, 8, 7)
    gate_rest = gate_of - gate_high
    gate_mid = lax.reduce_precision(gate_rest, 8, 7)
    info = jnp.stack([code, gate_high, gate_mid, gate_rest - gate_mid]).astype(BF)
    info = info.transpose(3, 0, 1, 2).reshape(-1, rows_local)

    query_cols = query_weight.shape[1]
    down_cols = latent_down.shape[1]
    out_rows = output_weight.shape[0]
    rank_local = latent_up.shape[0]
    up_rows = rank_local * latent_up.shape[1] // rows_local
    heads_dev = query_cols // (NOPE + ROPE)
    rows = Rows(out_rows, query_cols, up_rows, info.shape[0])
    straight = rows_local % 128 == 0
    query_t = query_weight.T.reshape(heads_dev, NOPE + ROPE, rows_local)
    rope_t = query_t[:, NOPE:].reshape(heads_dev, 2, ROPE // 2, rows_local).transpose(1, 0, 2, 3)
    gains = jnp.stack([attn_gain, ffn_gain, jnp.pad(latent_gain, (0, rows_local - rank_local))])
    packed = jnp.concatenate(
        [
            output_weight,
            query_t[:, :NOPE].reshape(heads_dev * NOPE, rows_local),
            rope_t.reshape(heads_dev * ROPE, rows_local),
            latent_down.T,
            latent_up.reshape(up_rows, rows_local),
            info,
            jnp.pad(gains, ((0, 13), (0, 0))),
        ],
        0,
    )
    grad_rows = grad_low.reshape(tokens, width)
    own_blocks = first_hops(packed, folds, chips_x)
    own_blocks, to_chips, grad_rows = lax.optimization_barrier((own_blocks, to_chips, grad_rows))
    own_blocks = second_hops(own_blocks, folds, chips_x)
    blocks = own_blocks + [core_swap(one, folds, chips_x) for one in own_blocks]
    order = jnp.stack(
        [
            ((core != side).astype(jnp.int32) * folds + (fold_at - f) % folds) * chips_x
            + (ctx_at // 2 - x) % chips_x
            for f in range(folds)
            for x in range(chips_x)
            for side in range(2)
        ]
    )

    def in_order(parts):
        return jnp.take(jnp.stack(parts), order, axis=0)

    def by_shift(parts):
        came = jnp.stack(
            [
                2 * (((fold_at - df) % folds) * chips_x + (ctx_at // 2 - dx) % chips_x) + side
                for side in (core, 1 - core)
                for df in range(folds)
                for dx in range(chips_x)
            ]
        )
        return jnp.take(parts, came, axis=0)

    up_full = in_order([one[rows.rope : rows.up] for one in blocks])
    up_full = up_full.reshape(RANK, latent_up.shape[1])
    gain_all = in_order([one[rows.info : rows.info + 3] for one in blocks])
    gain_two = gain_all[:, 1].reshape(width).astype(F32)
    lat_gain = gain_all[:, 2, :rank_local].reshape(RANK).astype(F32)
    info_all = jnp.stack([one[rows.up : rows.info] for one in own_blocks])
    if not straight:
        blocks = [in_order(blocks).transpose(1, 0, 2).reshape(rows.total, width)]
    count, piece = len(blocks), blocks[0].shape[1]
    info_all = info_all.reshape(chips, EXPERTS, 4, tokens)
    info_all = lax.dynamic_slice_in_dim(info_all, chip_at * per_chip, per_chip, 1).astype(F32)
    info_all = jnp.pad(info_all, ((0, 0), (0, -per_chip % 8), (0, 0), (0, 0)))
    code_all = info_all[:, :, 0]
    gate_all = info_all[:, :, 1] + info_all[:, :, 2] + info_all[:, :, 3]

    total_len = block * n_ctx
    inverse = 10000.0 ** (-jnp.arange(ROPE // 2, dtype=F32) / (ROPE // 2))
    angles = positions.astype(F32)[:, None] * inverse[None, :]
    cosine = jnp.tile(jnp.cos(angles), (seq_dev, 4))
    sine = jnp.tile(jnp.sin(angles), (seq_dev, 4))
    hidden_rows = hidden_in.reshape(tokens, width)
    side = heads_dev * ROPE
    low_one, q_nope, q_rope, key_rows, latent = one_step(
        functools.partial(project_kernel, rows, count),
        "project",
        [hidden_rows, lat_gain[None], cosine, sine] + blocks,
        [
            ((tokens, width), BF),
            ((tokens, heads_dev * NOPE), BF),
            ((tokens, side), BF),
            ((tokens, RANK + 128), BF),
            ((tokens, RANK), F32),
        ],
        [
            pltpu.VMEM((tokens, query_cols), F32),
            pltpu.VMEM((tokens, 256), F32),
            pltpu.VMEM((tokens, width), F32),
        ],
        2 * tokens * width * (query_cols + RANK + 256),
    )
    keys_all = row_gather(key_rows.reshape(seq_dev, block, RANK + 128), folds, chips_x)
    pieces = list(pieces_for(to_chips, folds, chips_x))
    from_chips = {
        (df, dx): chip_shift(one, folds, chips_x, df, dx)
        for one, df, dx in pieces
        if df == 0 or dx == 0
    }
    g_along = [chip_shift(grad_rows, folds, chips_x, df, 0) for df in range(folds)]
    late = [one for one in pieces if one[1] != 0 and one[2] != 0]
    late, grad_again, keys_all, from_chips = lax.optimization_barrier(
        ([one for one, _, _ in late], grad_rows, keys_all, from_chips)
    )
    at_once = from_chips
    late = {
        (df, dx): chip_shift(one, folds, chips_x, df, dx)
        for one, (df, dx) in zip(late, [at[1:] for at in pieces if at[1] != 0 and at[2] != 0])
    }
    attn_part, attended, expanded, log_total = one_step(
        functools.partial(attend_kernel, rows, count, seq_dev, block, n_ctx),
        "attend",
        [q_nope, q_rope, keys_all, up_full] + [(one, rows.out) for one in blocks],
        [
            ((tokens, width), BF),
            ((tokens, out_rows), BF),
            ((seq_dev, total_len, up_full.shape[1]), BF),
            ((tokens, 128), F32),
        ],
        [pltpu.VMEM((total_len, 256), BF)],
        2 * tokens * total_len * (RANK * 4 + 384 * heads_dev),
        (lengths,),
    )
    attn_part = attn_part.reshape(seq_dev, block, width)
    input_f = hidden_in.astype(F32)
    attn_sum = lax.psum(attn_part, "tp")

    g_first = first_hops(grad_again, folds, chips_x, g_along)
    late, g_first, attn_sum = lax.optimization_barrier((late, g_first, attn_sum))
    swapped = {at: core_swap(one, folds, chips_x) for at, one in at_once.items()}
    swapped.update({at: core_swap(one, folds, chips_x) for at, one in late.items()})
    arrived = {**at_once, **late}
    shifts = [(df, dx) for df in range(folds) for dx in range(chips_x)]
    from_chips = [arrived[at] for at in shifts]
    from_other = [swapped[at] for at in shifts]
    if straight:
        chip_weights = tuple(from_chips + from_other)
    else:
        both = in_order(from_chips + from_other)
        chip_weights = (both.transpose(1, 0, 2).reshape(sizes.rows, width),)
    middle = input_f + attn_sum.astype(F32)
    scale_two = rms_scale(middle)
    low_two = (middle * scale_two * gain_two).astype(BF)

    in_parts, out_parts = [], []

    def run_chunk(number, x_rows, g_rows, saved):
        part_in, part_out, *saved = chunk_call(
            sizes,
            number,
            chip_weights,
            code_all[number],
            gate_all[number],
            x_rows,
            g_rows,
            saved,
        )
        in_parts.append(part_in)
        out_parts.append(part_out)
        return saved

    own_rows = low_two.reshape(tokens, width)
    x_first = first_hops(own_rows, folds, chips_x)
    saved = run_chunk(0, own_rows, g_first[0, 0], None)
    x_first, g_first, saved = lax.optimization_barrier((x_first, g_first, saved))
    x_chunks = second_hops(x_first, folds, chips_x)
    g_chunks = second_hops(g_first, folds, chips_x)
    for number in range(1, chips):
        saved = run_chunk(number, x_chunks[number], g_chunks[number], saved)
    acts, shared_acts = saved

    def send(parts):
        return [
            chip_shift(parts[df * chips_x + dx], folds, chips_x, -df, -dx)
            for df in range(folds)
            for dx in range(chips_x)
        ]

    def total(parts):
        return sum(part.astype(F32) for part in parts).astype(BF).reshape(seq_dev, block, width)

    in_home = send(in_parts)
    ffn_g = weight_grad_call(
        sizes, rows_local, code_all, gate_all, acts, shared_acts, x_chunks, g_chunks
    )
    in_home, ffn_g = lax.optimization_barrier((in_home, ffn_g))
    in_sum = total(in_home)
    d_low_two = lax.psum(in_sum, "tp")
    in_sum, out_parts = lax.optimization_barrier((in_sum, out_parts))
    moe_low = total(send(out_parts))

    if straight:
        kept, given = ffn_g
    else:
        both = ffn_g[0].reshape(sizes.rows, chips, 2, rows_local).transpose(2, 1, 0, 3)
        kept = lax.dynamic_index_in_dim(both, core, 0, False)
        given = lax.dynamic_index_in_dim(both, 1 - core, 0, False)
    given = core_swap(given, folds, chips_x)
    moe_low, d_low_two = lax.optimization_barrier((moe_low, d_low_two))
    d_low_two = d_low_two.astype(F32)
    ffn_gain_g = jnp.sum(d_low_two * middle * scale_two, axis=(0, 1))
    d_middle = grad_out + norm_back(middle, scale_two, gain_two, d_low_two)
    d_branch = d_middle.astype(BF)
    d_branch = d_branch.reshape(tokens, width)
    d_query_pre, d_query_in, d_keys_part, latent_up_g = one_step(
        functools.partial(attend_back_kernel, rows, count, seq_dev, block, n_ctx),
        "attend_back",
        [d_branch, q_nope, q_rope, keys_all, expanded, log_total, up_full, cosine, sine]
        + [(one, rows.query) for one in blocks],
        [
            ((tokens, query_cols), BF),
            ((tokens, width), BF),
            ((n_ctx, seq_dev, block, RANK + 128), BF),
            ((RANK, up_full.shape[1]), F32),
        ],
        [
            pltpu.VMEM((tokens, out_rows), BF),
            pltpu.VMEM((total_len, up_full.shape[1]), BF),
            pltpu.VMEM((total_len, 256), BF),
            pltpu.VMEM((total_len, 256), F32),
            pltpu.VMEM((tokens, out_rows), F32),
        ],
        4 * tokens * total_len * (RANK * 4 + 384 * heads_dev),
        (lengths,),
    )
    d_keys_ctx = row_reduce(d_keys_part, folds, chips_x).astype(BF)
    d_query_in, d_keys_ctx, kept, given = lax.optimization_barrier(
        (d_query_in, d_keys_ctx, kept, given)
    )
    d_keys, d_query_sum = lax.psum((d_keys_ctx, d_query_in), "tp")
    ffn_sum = (kept.astype(F32) + given.astype(F32)).astype(BF)
    ffn_home = lax.all_to_all(
        ffn_sum, PLANE, split_axis=0, concat_axis=0, axis_index_groups=same_core, tiled=True
    ).astype(F32)
    d_keys, d_query_sum, d_query_pre, moe_low = lax.optimization_barrier(
        (d_keys, d_query_sum, d_query_pre, moe_low)
    )
    moe_sum = lax.psum(moe_low, "tp")

    def relayed(parts):
        if straight:
            return parts
        return by_shift(parts[0].reshape(-1, plane, rows_local).transpose(1, 0, 2))

    d_keys = d_keys.reshape(tokens, RANK + 128).astype(F32)
    d_lat_keys = d_keys[:, :RANK]
    scale_lat = rms_scale(latent)
    latent_gain_g = jnp.sum(d_lat_keys * latent * scale_lat, axis=0)
    d_latent = norm_back(latent, scale_lat, lat_gain, d_lat_keys)
    first = d_keys[:, RANK : RANK + ROPE // 2]
    second = d_keys[:, RANK + ROPE // 2 : RANK + ROPE]
    cosine, sine = cosine[:, : ROPE // 2], sine[:, : ROPE // 2]
    d_latent_pre = jnp.concatenate(
        [
            d_latent,
            first * cosine + second * sine,
            second * cosine - first * sine,
            jnp.zeros((tokens, 128 - ROPE), F32),
        ],
        -1,
    ).astype(BF)
    input_grad, packed_b = one_step(
        functools.partial(last_kernel, rows, count),
        "last_norm",
        [
            hidden_rows,
            low_one,
            d_query_sum.reshape(tokens, width),
            d_latent_pre,
            d_middle.reshape(tokens, width),
        ]
        + blocks,
        [((tokens, width), F32), ((count, down_cols + 16, piece), BF)],
        [pltpu.VMEM((tokens, width), F32)],
        4 * tokens * width * (RANK + 128),
    )
    packed_b, d_query_pre = lax.optimization_barrier((packed_b, d_query_pre))
    input_grad = input_grad.reshape(seq_dev, block, width)
    packed_b = relayed(packed_b)
    gain_rows = by_shift(latent_gain_g.astype(BF).reshape(plane, rank_local))
    packed_b = packed_b.at[:, down_cols + 1, :rank_local].set(gain_rows)
    own_b = plane_reduce(packed_b, folds, chips_x)
    down_s = own_b[:down_cols].T
    attn_gain_s = own_b[down_cols]
    lat_gain_s = own_b[down_cols + 1, :rank_local]

    grads_a = one_step(
        functools.partial(attend_grads_kernel, rows, count, piece),
        "attend_grads",
        [attended, d_branch, d_query_pre, low_one],
        [((count, rows.query, piece), BF)],
        [],
        2 * tokens * width * rows.query,
    )[0]
    small_a = jnp.concatenate(
        [
            latent_up_g.astype(BF).reshape(plane, up_rows, rows_local),
            ffn_gain_g.astype(BF).reshape(plane, 1, rows_local),
            jnp.zeros((plane, 15, rows_local), BF),
        ],
        1,
    )
    packed_a = jnp.concatenate([relayed(grads_a), by_shift(small_a)], 1)
    own_a = plane_reduce(packed_a, folds, chips_x)
    query_own = own_a[rows.out : rows.query]
    rope_own = query_own[heads_dev * NOPE :].reshape(2, heads_dev, ROPE // 2, rows_local)
    query_s = jnp.concatenate(
        [
            query_own[: heads_dev * NOPE].reshape(heads_dev, NOPE, rows_local),
            rope_own.transpose(1, 0, 2, 3).reshape(heads_dev, ROPE, rows_local),
        ],
        1,
    ).reshape(query_cols, rows_local)
    query_s = query_s.T
    output_s = own_a[: rows.out]
    up_s = own_a[rows.query : rows.query + up_rows].reshape(rank_local, -1)
    ffn_gain_s = own_a[rows.query + up_rows]

    gate_up_grad = ffn_home[:, : sizes.row_a].reshape(EXPERTS, 2, units, rows_local)
    gate_up_grad = gate_up_grad.transpose(3, 0, 1, 2)
    down_grad = ffn_home[:, sizes.row_a : sizes.row_b].reshape(EXPERTS, units, rows_local)
    down_grad = down_grad.transpose(2, 0, 1)
    shared_gu_s = (
        ffn_home[:, sizes.row_b : sizes.row_c]
        .reshape(chips, 2, sizes.part, rows_local)[:, :, :shared_part]
        .transpose(3, 1, 0, 2)
        .reshape(rows_local, 2, shared_units)
    )
    shared_down_s = ffn_home[:, sizes.row_c :][:, :shared_part].reshape(shared_units, rows_local)
    moe_sum, gate_up_grad, down_grad = lax.optimization_barrier((moe_sum, gate_up_grad, down_grad))
    block_out = (middle + moe_sum.astype(F32)).astype(BF)
    return (
        block_out,
        input_grad,
        attn_gain_s,
        query_s,
        down_s,
        lat_gain_s,
        up_s,
        output_s,
        ffn_gain_s,
        shared_gu_s,
        shared_down_s,
        gate_up_grad,
        down_grad,
    )


def solution(mesh):
    placed = (
        P("fsdp", "ctx", None),
        P("fsdp"),
        P("fsdp", "ctx", None),
        P("fsdp", "ctx", None),
        P("fsdp", "ctx", None),
        P(("fsdp", "ctx")),
        P(("fsdp", "ctx"), "tp"),
        P(("fsdp", "ctx"), None),
        P(("fsdp", "ctx")),
        P(("fsdp", "ctx"), "tp"),
        P("tp", ("fsdp", "ctx")),
        P(("fsdp", "ctx")),
        P(("fsdp", "ctx"), None, "tp"),
        P("tp", ("fsdp", "ctx")),
        P(("fsdp", "ctx"), None, None, "tp"),
        P(("fsdp", "ctx"), None, "tp"),
    )
    return jax.shard_map(
        local,
        mesh=mesh,
        in_specs=placed,
        out_specs=(
            P("fsdp", "ctx", None),
            P("fsdp", "ctx", None),
            P(("fsdp", "ctx")),
            P(("fsdp", "ctx"), "tp"),
            P(("fsdp", "ctx"), None),
            P(("fsdp", "ctx")),
            P(("fsdp", "ctx"), "tp"),
            P("tp", ("fsdp", "ctx")),
            P(("fsdp", "ctx")),
            P(("fsdp", "ctx"), None, "tp"),
            P("tp", ("fsdp", "ctx")),
            P(("fsdp", "ctx"), None, None, "tp"),
            P(("fsdp", "ctx"), None, "tp"),
        ),
        check_vma=False,
    )
```
